1024 devices in a mesh: dp: 32 (over y_hi, z), mp: 32 (over x, y_lo, core).
Axes of the slice: x: 4, y: 8 (y_hi: 2, y_lo: 4; y = y_hi * 4 + y_lo), z: 16, core: 2. Of those that a mesh axis runs over, the one named last changes fastest.
Arguments:
- inputs: bfloat16 [16384, 3072], P(('dp', 'mp')), may hold values from -600 to 600
- gain: float32 [3072], replicated, may hold values from 0.1 to 1.9
- qkv_weight: bfloat16 [3072, 32, 384], P(None, 'mp'), may hold values from -0.5 to 0.5
- d_attended: bfloat16 [16384, 32, 128], P('dp', 'mp'), may hold values from -6 to 6
Outputs:
- attended: bfloat16 [16384, 32, 128], P('dp', 'mp')
- input_grad: bfloat16 [16384, 3072], P(('dp', 'mp'))
- weight_grad: float32 [3072, 32, 384], P('dp', 'mp')
The draws below stay inside these ranges and needn't reach their ends.
All inputs are finite; a program needn't handle non-finite values.
Results may differ from the reference program's by a relative error of at most 0.04.
The reference program's roundings to bfloat16 on the way count: a program that leaves them out, or rounds other values in their place, can miss the bound.
Values may be sent and summed in bfloat16 or wider, within the bound.
A program may use at most 32 MiB of HBM per device.

```python
import math
import jax
import jax.numpy as jnp
from jax import lax

D = 3072
HD = 128
HEAD_DEV = 1
PATCHES = 256
IMG_GROUP = 2
HEADS = 32
TOK_GROUP = 512
TOKENS = 16384
N_DP = 32
N_MP = 32


def draw_inputs(key, part):
    key = jax.random.fold_in(key, 1)
    key_rows, key_cols, key_noise = jax.random.split(key, 3)
    row_scale = jnp.exp(jax.random.uniform(key_rows, (TOKENS, 1), minval=0.0, maxval=math.log(10.0)))
    col_scale = jnp.exp(jax.random.uniform(key_cols, (1, D), minval=0.0, maxval=math.log(10.0)))
    noise = jnp.clip(jax.random.normal(key_noise, (TOKENS, D)), -5.7, 5.7)
    return (row_scale * col_scale * noise).astype(jnp.float32).astype(jnp.bfloat16)


def draw_qkv_weight(key, part):
    key = jax.random.fold_in(key, 2)
    key_base = jax.random.fold_in(key, 0)
    base = jnp.clip(jax.random.normal(key_base, (D, HEADS, 3 * HD)), -5.0, 5.0) * D ** (-0.5)
    return base.astype(jnp.float32).astype(jnp.bfloat16)


def block_levels(rng, dims, pieces, least, largest):
    def one(axis_at, shards_of):
        draws = jax.random.uniform(jax.random.fold_in(jax.random.fold_in(rng, 6), axis_at), (shards_of,), jnp.float32, least / len(pieces), largest / len(pieces))
        return jnp.repeat(jnp.exp(draws), dims[axis_at] // shards_of).reshape((-1,) + (1,) * (len(dims) - axis_at - 1))

    factor_of = one(*pieces[0])
    for cut in pieces[1:]:
        factor_of = factor_of * one(*cut)
    return factor_of


def scatter_about(own_key, dims, deviation, limit, cuts=(), held_as=jnp.bfloat16):
    level = block_levels(own_key, dims, cuts, -0.22, 0.18) if cuts else 1.0
    values = jax.random.normal(own_key, dims, jnp.float32) * deviation * level
    return jnp.minimum(jnp.maximum(values, -limit), limit).astype(held_as)


def setup_inputs(seed: int = 0) -> dict:
    splits = jax.random.split(jax.random.key(seed), 5)
    inputs = draw_inputs(jax.random.fold_in(splits[4], 71), 0)
    gain = jnp.clip(1.0 + 0.18 * jax.random.normal(splits[1], (D,), jnp.float32), 0.1, 1.9)
    qkv_weight = draw_qkv_weight(jax.random.fold_in(splits[4], 71), 0)
    d_attended = scatter_about(splits[3], (TOKENS, HEADS, HD), 1.0, 6.0, ((0, 32), (1, 32)))
    return {"inputs": inputs, "gain": gain, "qkv_weight": qkv_weight, "d_attended": d_attended}


def normalize(rows, gain):
    mean = lax.optimization_barrier(jnp.mean(rows, -1, keepdims=True))
    centered = rows - mean
    spread = lax.optimization_barrier(jnp.mean(centered * centered, -1, keepdims=True))
    return centered * lax.rsqrt(spread + 1e-06) * gain.astype(jnp.float32)

def attend(block, d_out):
    scale = HD ** (-0.5)
    query = block[:, :HD].astype(jnp.float32)
    keys = block[:, HD:2 * HD].astype(jnp.float32)
    values = block[:, 2 * HD:].astype(jnp.float32)
    scores = jnp.dot(query, keys.T) * scale
    peak = lax.optimization_barrier(jnp.max(scores, -1, keepdims=True))
    expo = jnp.exp(scores - peak)
    probs = expo / lax.optimization_barrier(jnp.sum(expo, -1, keepdims=True))
    probs_low = probs.astype(jnp.bfloat16).astype(jnp.float32)
    output = jnp.dot(probs_low, values).astype(jnp.bfloat16)
    d_outf = d_out.astype(jnp.float32)
    d_probs = jnp.dot(d_outf, values.T)
    d_values = jnp.dot(probs_low.T, d_outf)
    d_scores = (probs * (d_probs - lax.optimization_barrier(jnp.sum(d_probs * probs, -1, keepdims=True))) * scale).astype(jnp.bfloat16).astype(jnp.float32)
    d_query = jnp.dot(d_scores, keys)
    d_keys = jnp.dot(d_scores.T, query)
    return (output, jnp.concatenate([d_query, d_keys, d_values], -1).astype(jnp.bfloat16))

def reference(inputs, gain, qkv_weight, d_attended):
    weight = qkv_weight.astype(jnp.float32).reshape(D, HEADS * 3 * HD)
    weight_sets = weight.reshape(D, N_MP, HEAD_DEV * 3 * HD)
    groups_in = inputs.reshape(N_DP, TOK_GROUP, D)
    groups_d = d_attended.reshape(N_DP, TOK_GROUP, HEADS, HD)
    per_image = jax.vmap(jax.vmap(attend, in_axes=(1, 1), out_axes=(1, 1)))

    def step(total, pair):
        in_group, d_group = pair
        normed32, back = jax.vjp(lambda r: normalize(r, gain), in_group.astype(jnp.float32))
        normed = normed32.astype(jnp.bfloat16).astype(jnp.float32)
        qkv = jnp.dot(normed, weight).astype(jnp.bfloat16)
        qkv = qkv.reshape(IMG_GROUP, PATCHES, HEADS, 3 * HD)
        d_out = d_group.reshape(IMG_GROUP, PATCHES, HEADS, HD)
        output, d_qkv = per_image(qkv, d_out)
        d_flat = d_qkv.reshape(TOK_GROUP, HEADS * 3 * HD).astype(jnp.float32)
        grad_term = jnp.dot(normed.T, d_flat).astype(jnp.bfloat16)
        grad_term = lax.optimization_barrier(grad_term).astype(jnp.float32)
        d_sets = d_flat.reshape(TOK_GROUP, N_MP, HEAD_DEV * 3 * HD)
        terms = jnp.einsum('tme,dme->mtd', d_sets, weight_sets).astype(jnp.bfloat16)
        terms = lax.optimization_barrier(terms).astype(jnp.float32)
        d_normed = lax.optimization_barrier(jnp.sum(terms, 0))
        in_back = back(d_normed)[0].astype(jnp.bfloat16)
        return (total + grad_term, (output.reshape(TOK_GROUP, HEADS, HD), in_back))
    start = jnp.zeros((D, HEADS * 3 * HD), jnp.float32)
    total, (outputs, in_backs) = lax.scan(step, start, (groups_in, groups_d))
    return (outputs.reshape(TOKENS, HEADS, HD), in_backs.reshape(TOKENS, D), total.reshape(D, HEADS, 3 * HD))
```

```python
import jax
import jax.numpy as jnp
from jax import lax
from jax.experimental import pallas as pl
from jax.experimental.pallas import tpu as pltpu
from jax.sharding import PartitionSpec as P

MESH = pl.DeviceIdType.MESH
BF16, F32 = jnp.bfloat16, jnp.float32

NX, NY, NC, NZ, NH = 4, 4, 2, 16, 2
ROWS, D, HD = 16, 3072, 128
QKV = 3 * HD
GROUP = NX * NY * NC * ROWS
IMAGE = GROUP // 2
HALF = D // 2
OWN = D // (NZ * NH)
RIGHT_STEPS, LEFT_STEPS = NZ // 2, NZ // 2 - 1
TILE = 4 * OWN


def mod(a, n):
    return lax.rem(a, jnp.int32(n))


def div(a, n):
    return lax.div(a, jnp.int32(n))


def dot(a, b, ca, cb):
    return lax.dot_general(a, b, (((ca,), (cb,)), ((), ())), preferred_element_type=F32)


def arrived(ref, sem):
    pltpu.make_async_copy(ref, ref, sem).wait()


def kernel(
    in_ref, gain_ref, w_hbm, do_hbm,
    att_ref, ing_ref, wg_ref,
    w, do, normed, qkv, dqkv, grads, terms, from_core, half_l, half_r, full_l, full_r, from_y,
    zin_r, zin_l, yh_out, yh_in,
    sem_w, sem_do, sem_y, sem_xl, sem_xr, sem_x2l, sem_x2r, sem_sib,
    sem_zr, sem_zl, sem_core, sem_hl, sem_hr, sem_fl, sem_fr, sem_fy, sem_yh,
    out_ag, out_z, out_mp, out_yh,
):
    dp, mp = lax.axis_index("dp"), lax.axis_index("mp")
    x, y, c = div(mp, 8), mod(div(mp, 2), 4), mod(mp, 2)
    h, z = div(dp, NZ), mod(dp, NZ)
    xr, xl, xo = mod(x + 1, NX), mod(x + 3, NX), mod(x + 2, NX)
    other_c, other_h = 1 - c, 1 - h
    near = [y, y + 1 - 2 * mod(y, 2), mod(y + 2, NY), NY - 1 - y]

    def at_mp(xx, yy, cc):
        return (dp, xx * 8 + yy * 2 + cc)

    to_right, to_left = at_mp(xr, y, c), at_mp(xl, y, c)
    to_sib = at_mp(x, y, other_c)
    to_zr, to_zl = (h * NZ + mod(z + 1, NZ), mp), (h * NZ + mod(z + NZ - 1, NZ), mp)
    to_yh = (other_h * NZ + z, mp)

    def send(src, dst, out_sem, in_sem, device):
        pltpu.make_async_remote_copy(
            src_ref=src, dst_ref=dst, send_sem=out_sem, recv_sem=in_sem, device_id=device, device_id_type=MESH
        ).start()

    barrier = pltpu.get_barrier_semaphore()
    partners = [to_right, to_left, to_sib, to_zr, to_zl, to_yh] + [at_mp(x, near[k], c) for k in (1, 2, 3)]
    for device in partners:
        pl.semaphore_signal(barrier, inc=1, device_id=device, device_id_type=MESH)
    load_w = pltpu.make_async_copy(w_hbm, w, sem_w)
    load_w.start()
    load_do = pltpu.make_async_copy(do_hbm, do, sem_do)
    load_do.start()

    rows = in_ref[...].astype(F32)
    gain = gain_ref[...]
    mean = jnp.sum(rows, -1, keepdims=True) * (1.0 / D)
    centered = rows - mean
    inv = lax.rsqrt(jnp.sum(centered * centered, -1, keepdims=True) * (1.0 / D) + 1e-6)
    normed[x, y, c] = (centered * inv * gain).astype(BF16)

    pl.semaphore_wait(barrier, len(partners))

    def to_sibling(ref, slot):
        send(ref, ref, out_ag, sem_sib.at[slot], to_sib)

    def along_x(yy):
        block = normed.at[x, yy, c]
        send(block, block, out_ag, sem_xl.at[yy], to_right)
        send(block, block, out_ag, sem_xr.at[yy], to_left)

    own = normed.at[x, y, c]
    along_x(y)
    for k in (1, 2, 3):
        send(own, own, out_ag, sem_y.at[y], at_mp(x, near[k], c))
    to_sibling(own, 0)
    for k in range(NY):
        if k + 1 < NY:
            yy = near[k + 1]
            arrived(normed.at[x, yy, c], sem_y.at[yy])
            along_x(yy)
            to_sibling(normed.at[x, yy, c], 0)
        yy = near[k]
        block = normed.at[xl, yy, c]
        arrived(block, sem_xl.at[yy])
        piece = block.at[:, pl.ds(0, HALF)]
        send(piece, piece, out_ag, sem_x2l.at[yy], to_right)
        to_sibling(block, 1)
        block = normed.at[xr, yy, c]
        arrived(block, sem_xr.at[yy])
        piece = block.at[:, pl.ds(HALF, HALF)]
        send(piece, piece, out_ag, sem_x2r.at[yy], to_left)
        to_sibling(block, 2)

    def project(xx):
        qkv[xx] = dot(normed[xx].reshape(IMAGE // 2, D), w[...], 1, 0).astype(BF16)

    def second(k):
        yy = near[k]
        piece = normed.at[xo, yy, c, :, pl.ds(0, HALF)]
        arrived(piece, sem_x2l.at[yy])
        to_sibling(piece, 3)
        piece = normed.at[xo, yy, c, :, pl.ds(HALF, HALF)]
        arrived(piece, sem_x2r.at[yy])
        to_sibling(piece, 3)

    def bundle(xx, slot):
        arrived(normed.at[xx, :, other_c], sem_sib.at[slot])

    def attend(a):
        block = qkv[pl.ds(2 * a, 2)].reshape(IMAGE, QKV)
        q, k, v = block[:, :HD], block[:, HD : 2 * HD], block[:, 2 * HD :]
        d_out = do[a]
        scale = HD ** (-0.5)
        scores = dot(q, k, 1, 1) * scale
        expo = jnp.exp(scores - jnp.max(scores, -1, keepdims=True))
        probs = expo / jnp.sum(expo, -1, keepdims=True)
        low = probs.astype(BF16)
        att_ref[a] = dot(low, v, 1, 0).astype(BF16)
        d_probs = dot(d_out, v, 1, 1)
        dqkv[a, :, 2 * HD :] = dot(low, d_out, 0, 0).astype(BF16)
        d_scores = (probs * (d_probs - jnp.sum(d_probs * probs, -1, keepdims=True)) * scale).astype(BF16)
        dqkv[a, :, :HD] = dot(d_scores, k, 1, 0).astype(BF16)
        dqkv[a, :, HD : 2 * HD] = dot(d_scores, q, 0, 0).astype(BF16)

    load_w.wait()
    load_do.wait()
    bundle(x, 0)
    project(x)
    second(0)
    second(1)
    bundle(xl, 1)
    bundle(xr, 2)
    image = div(x, 2)
    mate = x + 1 - 2 * mod(x, 2)
    project(mate)
    second(2)
    second(3)
    attend(image)
    project(mod(mate + 2, NX))
    bundle(xo, 3)
    project(xo)
    attend(1 - image)

    def grad_tile(t):
        u = mod(t, 4)
        d_all = dqkv[...].reshape(GROUP, QKV)
        for hh in range(NH):
            cols = pl.ds(pl.multiple_of((u + 4 * hh) * TILE, 128), TILE)
            tile = normed[:, :, :, :, cols].reshape(GROUP, TILE)
            grads[hh, pl.ds(4 * u, 4)] = dot(tile, d_all, 0, 0).astype(BF16).reshape(4, OWN, QKV)

    subs = (other_h, h)

    def z_right(s):
        zz = mod(z + 8 - s + NZ, NZ)
        for sub in range(2):
            block = grads.at[subs[sub], zz]
            if s > 0:
                arrived(zin_r.at[s - 1, sub], sem_zr.at[s - 1, sub])
                block[...] = (block[...].astype(F32) + zin_r[s - 1, sub].astype(F32)).astype(BF16)
            send(block, zin_r.at[s, sub], out_z, sem_zr.at[s, sub], to_zr)

    def z_left(s):
        zz = mod(z + 9 + s, NZ)
        for sub in range(2):
            block = grads.at[subs[sub], zz]
            if s > 0:
                arrived(zin_l.at[s - 1, sub], sem_zl.at[s - 1, sub])
                block[...] = (block[...].astype(F32) + zin_l[s - 1, sub].astype(F32)).astype(BF16)
            send(block, zin_l.at[s, sub], out_z, sem_zl.at[s, sub], to_zl)

    def z_step(s):
        z_right(s)
        if s < LEFT_STEPS:
            z_left(s)

    first = div(mod(z + 8, NZ), 4)
    grad_tile(first)
    grad_tile(first + 1)
    z_step(0)
    grad_tile(first + 3)
    grad_tile(first + 2)

    def share(j, carry):
        cols = pl.ds(pl.multiple_of(j * 256, 256), 256)
        out = dot(dqkv[...].reshape(GROUP, QKV), w[cols, :], 1, 1).astype(BF16)
        terms[:, :, :, :, cols] = out.reshape(NX, NY, NC, ROWS, 256)
        return carry

    lax.fori_loop(0, D // 256, share, 0)
    order = (xo, xr, xl, x)
    for j in range(NX):
        send(terms.at[order[j], :, other_c], from_core.at[j], out_mp, sem_core.at[j], to_sib)
    z_step(1)

    ys = [mod(y + 1, NY), mod(y + 2, NY), mod(y + 3, NY), y]

    def both_cores(j, k):
        return terms[order[j], ys[k], c].astype(F32) + from_core[j, ys[k]].astype(F32)

    def start_x(k):
        block = terms.at[xo, ys[k], c]
        block[...] = both_cores(0, k).astype(BF16)
        send(block.at[:, pl.ds(0, HALF)], half_l.at[k], out_mp, sem_hl.at[k], to_right)
        send(block.at[:, pl.ds(HALF, HALF)], half_r.at[k], out_mp, sem_hr.at[k], to_left)

    def relay_x(k):
        total = both_cores(1, k)
        block = terms.at[xr, ys[k], c]
        arrived(half_l.at[k], sem_hl.at[k])
        block[:, :HALF] = (total[:, :HALF] + half_l[k].astype(F32)).astype(BF16)
        block[:, HALF:] = total[:, HALF:].astype(BF16)
        send(block, full_l.at[k], out_mp, sem_fl.at[k], to_right)
        total = both_cores(2, k)
        block = terms.at[xl, ys[k], c]
        arrived(half_r.at[k], sem_hr.at[k])
        block[:, :HALF] = total[:, :HALF].astype(BF16)
        block[:, HALF:] = (total[:, HALF:] + half_r[k].astype(F32)).astype(BF16)
        send(block, full_r.at[k], out_mp, sem_fr.at[k], to_left)

    def end_x(k):
        total = both_cores(3, k)
        arrived(full_l.at[k], sem_fl.at[k])
        arrived(full_r.at[k], sem_fr.at[k])
        total = total + full_l[k].astype(F32) + full_r[k].astype(F32)
        if k == NY - 1:
            return total
        block = terms.at[x, ys[k], c]
        block[...] = total.astype(BF16)
        send(block, from_y.at[y], out_mp, sem_fy.at[y], at_mp(x, ys[k], c))
        return None

    arrived(from_core.at[0], sem_core.at[0])
    for k in range(NY):
        start_x(k)
    z_step(2)
    arrived(from_core.at[1], sem_core.at[1])
    arrived(from_core.at[2], sem_core.at[2])
    relay_x(0)
    relay_x(1)
    z_step(3)
    relay_x(2)
    relay_x(3)
    z_step(4)
    arrived(from_core.at[3], sem_core.at[3])
    end_x(0)
    end_x(1)
    z_step(5)
    end_x(2)
    d_normed = end_x(3)
    z_step(6)
    for k in range(NY - 1):
        arrived(from_y.at[ys[k]], sem_fy.at[ys[k]])
        d_normed = d_normed + from_y[ys[k]].astype(F32)
    rows = in_ref[...].astype(F32)
    centered = rows - jnp.sum(rows, -1, keepdims=True) * (1.0 / D)
    inv = lax.rsqrt(jnp.sum(centered * centered, -1, keepdims=True) * (1.0 / D) + 1e-6)
    hat = centered * inv
    grown = d_normed * gain_ref[...]
    lean = jnp.sum(grown * hat, -1, keepdims=True) * (1.0 / D)
    ing_ref[...] = (inv * (grown - jnp.sum(grown, -1, keepdims=True) * (1.0 / D) - hat * lean)).astype(BF16)
    z_step(7)

    def z_end(sub):
        arrived(zin_l.at[LEFT_STEPS - 1, sub], sem_zl.at[LEFT_STEPS - 1, sub])
        arrived(zin_r.at[RIGHT_STEPS - 1, sub], sem_zr.at[RIGHT_STEPS - 1, sub])
        return (
            grads[subs[sub], z].astype(F32)
            + zin_l[LEFT_STEPS - 1, sub].astype(F32)
            + zin_r[RIGHT_STEPS - 1, sub].astype(F32)
        )

    yh_out[...] = z_end(0).astype(BF16)
    send(yh_out, yh_in, out_yh, sem_yh, to_yh)
    total = z_end(1)
    arrived(yh_in, sem_yh)
    wg_ref[...] = total + yh_in[...].astype(F32)

    blocks = NX * NY * NC - 1
    for sem in (out_ag, out_mp):
        pltpu.make_async_copy(
            normed.at[pl.ds(0, 3)], normed.at[pl.ds(0, 3)], sem
        ).wait()
        pltpu.make_async_copy(normed.at[3, pl.ds(0, 3)], normed.at[3, pl.ds(0, 3)], sem).wait()
        pltpu.make_async_copy(normed.at[3, 3, 0], normed.at[3, 3, 0], sem).wait()
    assert blocks == 31
    pltpu.make_async_copy(grads.at[0], grads.at[0], out_z).wait()
    pltpu.make_async_copy(grads.at[1, pl.ds(0, 14)], grads.at[1, pl.ds(0, 14)], out_z).wait()
    pltpu.make_async_copy(yh_out, yh_out, out_yh).wait()


def local(inputs, gain, qkv_weight, d_attended):
    vmem, anywhere = pl.BlockSpec(memory_space=pltpu.VMEM), pl.BlockSpec(memory_space=pl.ANY)
    dma = pltpu.SemaphoreType.DMA
    blocks = (NX, NY, NC, ROWS, D)
    attended, input_grad, weight_grad = pl.pallas_call(
        kernel,
        out_shape=(
            jax.ShapeDtypeStruct((2, IMAGE, HD), BF16),
            jax.ShapeDtypeStruct((ROWS, D), BF16),
            jax.ShapeDtypeStruct((OWN, QKV), F32),
        ),
        in_specs=[vmem, vmem, anywhere, anywhere],
        out_specs=(vmem, vmem, vmem),
        scratch_shapes=[
            pltpu.VMEM((D, QKV), BF16),
            pltpu.VMEM((2, IMAGE, HD), BF16),
            pltpu.VMEM(blocks, BF16),
            pltpu.VMEM((NX, IMAGE // 2, QKV), BF16),
            pltpu.VMEM((2, IMAGE, QKV), BF16),
            pltpu.VMEM((NH, NZ, OWN, QKV), BF16),
            pltpu.VMEM(blocks, BF16),
            pltpu.VMEM((NX, NY, ROWS, D), BF16),
            pltpu.VMEM((NY, ROWS, HALF), BF16),
            pltpu.VMEM((NY, ROWS, HALF), BF16),
            pltpu.VMEM((NY, ROWS, D), BF16),
            pltpu.VMEM((NY, ROWS, D), BF16),
            pltpu.VMEM((NY, ROWS, D), BF16),
            pltpu.VMEM((RIGHT_STEPS, 2, OWN, QKV), BF16),
            pltpu.VMEM((LEFT_STEPS, 2, OWN, QKV), BF16),
            pltpu.VMEM((OWN, QKV), BF16),
            pltpu.VMEM((OWN, QKV), BF16),
            dma, dma,
            dma((NY,)), dma((NY,)), dma((NY,)), dma((NY,)), dma((NY,)), dma((4,)),
            dma((RIGHT_STEPS, 2)), dma((LEFT_STEPS, 2)),
            dma((NX,)), dma((NY,)), dma((NY,)), dma((NY,)), dma((NY,)), dma((NY,)), dma,
            dma, dma, dma, dma,
        ],
        compiler_params=pltpu.CompilerParams(
            collective_id=0, has_side_effects=True, vmem_limit_bytes=48 * 1024 * 1024
        ),
    )(inputs, gain.reshape(1, D), qkv_weight.reshape(D, QKV), d_attended.reshape(2, IMAGE, HD))
    return (attended.reshape(GROUP, 1, HD), input_grad, weight_grad.reshape(OWN, 1, QKV))


def solution(mesh):
    return jax.shard_map(
        local,
        mesh=mesh,
        in_specs=(P(("dp", "mp"), None), P(), P(None, "mp", None), P("dp", "mp", None)),
        out_specs=(P("dp", "mp", None), P(("dp", "mp"), None), P("dp", "mp", None)),
        check_vma=False,
    )
```

```python
import jax
import jax.numpy as jnp
from jax import lax
from jax.experimental import pallas as pl
from jax.experimental.pallas import tpu as pltpu
from jax.sharding import PartitionSpec as P

MESH = pl.DeviceIdType.MESH
STRAIGHT = (True, False, False, True)
Y_FIRST = (1, 2, 3)
Z_PARTS = 2
BF16, F32 = jnp.bfloat16, jnp.float32

NX, NY, NC, NZ, NH = 4, 4, 2, 16, 2
ROWS, D, HD = 16, 3072, 128
QKV = 3 * HD
GROUP = NX * NY * NC * ROWS
IMAGE = GROUP // 2
HALF = D // 2
OWN = D // (NZ * NH)
RIGHT_STEPS, LEFT_STEPS = NZ // 2, NZ // 2 - 1
PART = OWN // Z_PARTS
TILE = 4 * OWN


def mod(a, n):
    return lax.rem(a, jnp.int32(n))


def div(a, n):
    return lax.div(a, jnp.int32(n))


def dot(a, b, ca, cb):
    return lax.dot_general(a, b, (((ca,), (cb,)), ((), ())), preferred_element_type=F32)


def arrived(ref, sem):
    pltpu.make_async_copy(ref, ref, sem).wait()


def kernel(
    in_hbm, gain_hbm, w_hbm, do_hbm,
    att_hbm, ing_hbm, wg_hbm,
    att_ref, ing_ref, wg_ref,
    in_ref, gain_ref, w, do, normed, qkv, dqkv, grads, terms, from_core, half_l, half_r, full_l, full_r, from_y,
    zin_r, zin_l, yh_in,
    sem_in, sem_gain, sem_w, sem_do, sem_y, sem_xl, sem_xr, sem_xo, sem_x2l, sem_x2r, sem_sib,
    sem_zr, sem_zl, sem_core, sem_hl, sem_hr, sem_fl, sem_fr, sem_fy, sem_yh, sem_own, sem_att, sem_ing, sem_wg,
    out_ag, out_z, out_mp,
):
    dp, mp = lax.axis_index("dp"), lax.axis_index("mp")
    x, y, c = div(mp, 8), mod(div(mp, 2), 4), mod(mp, 2)
    h, z = div(dp, NZ), mod(dp, NZ)
    xr, xl, xo = mod(x + 1, NX), mod(x + 3, NX), mod(x + 2, NX)
    other_c, other_h = 1 - c, 1 - h
    near = [y, y + 1 - 2 * mod(y, 2), mod(y + 2, NY), NY - 1 - y]

    def at_mp(xx, yy, cc):
        return (dp, xx * 8 + yy * 2 + cc)

    to_right, to_left = at_mp(xr, y, c), at_mp(xl, y, c)
    to_sib, to_across = at_mp(x, y, other_c), at_mp(xo, y, c)
    to_zr, to_zl = (h * NZ + mod(z + 1, NZ), mp), (h * NZ + mod(z + NZ - 1, NZ), mp)
    over, over_zr, over_zl = ((other_h * NZ + mod(z + step, NZ), mp) for step in (0, 1, NZ - 1))

    def send(src, dst, out_sem, in_sem, device):
        pltpu.make_async_remote_copy(
            src_ref=src, dst_ref=dst, send_sem=out_sem, recv_sem=in_sem, device_id=device, device_id_type=MESH
        ).start()

    barrier = pltpu.get_barrier_semaphore()
    partners = [to_right, to_left, to_across, to_sib, to_zr, to_zl, over, over_zr, over_zl] + [at_mp(x, near[k], c) for k in (1, 2, 3)]
    for device in partners:
        pl.semaphore_signal(barrier, inc=1, device_id=device, device_id_type=MESH)
    load_in = pltpu.make_async_copy(in_hbm, in_ref, sem_in)
    load_in.start()
    load_gain = pltpu.make_async_copy(gain_hbm, gain_ref, sem_gain)
    load_gain.start()
    load_w = pltpu.make_async_copy(w_hbm, w, sem_w)
    load_w.start()
    load_do = pltpu.make_async_copy(do_hbm, do, sem_do)
    load_do.start()

    load_in.wait()
    load_gain.wait()
    rows = in_ref[...].astype(F32)
    gain = gain_ref[...]
    mean = jnp.sum(rows, -1, keepdims=True) * (1.0 / D)
    centered = rows - mean
    inv = lax.rsqrt(jnp.sum(centered * centered, -1, keepdims=True) * (1.0 / D) + 1e-6)
    normed[x, y, c] = (centered * inv * gain).astype(BF16)

    pl.semaphore_wait(barrier, len(partners))

    def to_sibling(ref, slot):
        send(ref, ref, out_ag, sem_sib.at[slot], to_sib)

    pieces = (pl.ds(0, HALF), pl.ds(HALF, HALF))

    def along_x(k):
        yy = near[k]
        block = normed.at[x, yy, c]
        for right, p in ((True, 0), (False, 1), (True, 1), (False, 0)):
            part = block.at[:, pieces[p]]
            sem, device = (sem_xl, to_right) if right else (sem_xr, to_left)
            send(part, part, out_ag, sem.at[yy, p], device)
        if STRAIGHT[k]:
            send(block, block, out_ag, sem_xo.at[yy], to_across)

    def along_y(k):
        send(own, own, out_ag, sem_y.at[y], at_mp(x, near[k], c))

    def pass_on(k):
        yy = near[k]
        if not STRAIGHT[k]:
            part = normed.at[xl, yy, c, :, pieces[0]]
            arrived(part, sem_xl.at[yy, 0])
            send(part, part, out_ag, sem_x2l.at[yy], to_right)
            part = normed.at[xr, yy, c, :, pieces[1]]
            arrived(part, sem_xr.at[yy, 1])
            send(part, part, out_ag, sem_x2r.at[yy], to_left)

    def finish_x(k):
        yy = near[k]
        if STRAIGHT[k]:
            arrived(normed.at[xl, yy, c, :, pieces[0]], sem_xl.at[yy, 0])
            arrived(normed.at[xr, yy, c, :, pieces[1]], sem_xr.at[yy, 1])
        arrived(normed.at[xl, yy, c, :, pieces[1]], sem_xl.at[yy, 1])
        to_sibling(normed.at[xl, yy, c], 1)
        arrived(normed.at[xr, yy, c, :, pieces[0]], sem_xr.at[yy, 0])
        to_sibling(normed.at[xr, yy, c], 2)

    own = normed.at[x, y, c]
    along_x(0)
    for k in Y_FIRST:
        along_y(k)
    to_sibling(own, 0)
    for k in range(NY):
        if k + 1 < NY:
            yy = near[k + 1]
            arrived(normed.at[x, yy, c], sem_y.at[yy])
            along_x(k + 1)
            to_sibling(normed.at[x, yy, c], 0)
        if k == 0:
            for j in (1, 2, 3):
                if j not in Y_FIRST:
                    along_y(j)
        pass_on(k)
        if k > 0:
            finish_x(k - 1)
    finish_x(NY - 1)

    def second(k):
        yy = near[k]
        if STRAIGHT[k]:
            block = normed.at[xo, yy, c]
            arrived(block, sem_xo.at[yy])
            to_sibling(block, 3)
            return
        for p, sem in ((0, sem_x2l), (1, sem_x2r)):
            part = normed.at[xo, yy, c, :, pieces[p]]
            arrived(part, sem.at[yy])
            to_sibling(part, 3)

    def bundle(xx, slot):
        arrived(normed.at[xx, :, other_c], sem_sib.at[slot])

    def project(xx):
        qkv[xx] = dot(normed[xx].reshape(IMAGE // 2, D), w[...], 1, 0).astype(BF16)

    def attend(a):
        block = qkv[pl.ds(2 * a, 2)].reshape(IMAGE, QKV)
        q, k, v = block[:, :HD], block[:, HD : 2 * HD], block[:, 2 * HD :]
        d_out = do[a]
        scale = HD ** (-0.5)
        scores = dot(q, k, 1, 1) * scale
        expo = jnp.exp(scores - jnp.max(scores, -1, keepdims=True))
        probs = expo / jnp.sum(expo, -1, keepdims=True)
        low = probs.astype(BF16)
        att_ref[a] = dot(low, v, 1, 0).astype(BF16)
        d_probs = dot(d_out, v, 1, 1)
        dqkv[a, :, 2 * HD :] = dot(low, d_out, 0, 0).astype(BF16)
        d_scores = (probs * (d_probs - jnp.sum(d_probs * probs, -1, keepdims=True)) * scale).astype(BF16)
        dqkv[a, :, :HD] = dot(d_scores, k, 1, 0).astype(BF16)
        dqkv[a, :, HD : 2 * HD] = dot(d_scores, q, 0, 0).astype(BF16)

    load_w.wait()
    load_do.wait()
    bundle(x, 0)
    project(x)
    second(0)
    second(1)
    bundle(xl, 1)
    bundle(xr, 2)
    image = div(x, 2)
    mate = x + 1 - 2 * mod(x, 2)
    project(mate)
    second(2)
    second(3)
    attend(image)
    project(mod(mate + 2, NX))
    bundle(xo, 3)
    project(xo)
    attend(1 - image)

    store_att = pltpu.make_async_copy(att_ref, att_hbm, sem_att)
    store_att.start()

    def grad_tile(t):
        u = mod(t, 4)
        d_all = dqkv[...].reshape(GROUP, QKV)
        for hh in range(NH):
            cols = pl.ds(pl.multiple_of((u + 4 * hh) * TILE, 128), TILE)
            tile = normed[:, :, :, :, cols].reshape(GROUP, TILE)
            grads[hh, pl.ds(4 * u, 4)] = dot(tile, d_all, 0, 0).astype(BF16).reshape(4, OWN, QKV)

    def z_part(s, sub, part, right):
        zz = mod(z + 8 - s + NZ, NZ) if right else mod(z + 9 + s, NZ)
        came, sem, device = (zin_r, sem_zr, to_zr) if right else (zin_l, sem_zl, to_zl)
        rows = pl.ds(part * PART, PART)
        block = grads.at[(other_h, h)[sub], zz, rows]
        if s > 0:
            arrived(came.at[s - 1, sub, rows], sem.at[s - 1, sub * Z_PARTS + part])
            block[...] = (block[...].astype(F32) + came[s - 1, sub, rows].astype(F32)).astype(BF16)
        last = s == (RIGHT_STEPS if right else LEFT_STEPS) - 1
        if last and sub == 0:
            slot = 1 if right else 2
            send(block, yh_in.at[slot, rows], out_z, sem_yh.at[slot, part], over_zr if right else over_zl)
        else:
            send(block, came.at[s, sub, rows], out_z, sem.at[s, sub * Z_PARTS + part], device)

    def z_step(s, ways=(True, False)):
        for sub in range(2):
            for part in range(Z_PARTS):
                for right in ways:
                    if right or s < LEFT_STEPS:
                        z_part(s, sub, part, right)

    def own_over():
        block = grads.at[other_h, z]
        send(block, yh_in.at[0], out_z, sem_own, over)

    def share(j, carry):
        cols = pl.ds(pl.multiple_of(j * 256, 256), 256)
        out = dot(dqkv[...].reshape(GROUP, QKV), w[cols, :], 1, 1).astype(BF16)
        terms[:, :, :, :, cols] = out.reshape(NX, NY, NC, ROWS, 256)
        return carry

    order = (xo, xr, xl, x)
    ys = [mod(y + 1, NY), mod(y + 2, NY), mod(y + 3, NY), y]

    def both_cores(j, k):
        return terms[order[j], ys[k], c].astype(F32) + from_core[j, ys[k]].astype(F32)

    def start_x(k):
        block = terms.at[xo, ys[k], c]
        block[...] = both_cores(0, k).astype(BF16)
        send(block.at[:, pl.ds(0, HALF)], half_l.at[k], out_mp, sem_hl.at[k], to_right)
        send(block.at[:, pl.ds(HALF, HALF)], half_r.at[k], out_mp, sem_hr.at[k], to_left)

    def relay_x(k):
        total = both_cores(1, k)
        block = terms.at[xr, ys[k], c]
        arrived(half_l.at[k], sem_hl.at[k])
        block[:, :HALF] = (total[:, :HALF] + half_l[k].astype(F32)).astype(BF16)
        block[:, HALF:] = total[:, HALF:].astype(BF16)
        send(block, full_l.at[k], out_mp, sem_fl.at[k], to_right)
        total = both_cores(2, k)
        block = terms.at[xl, ys[k], c]
        arrived(half_r.at[k], sem_hr.at[k])
        block[:, :HALF] = total[:, :HALF].astype(BF16)
        block[:, HALF:] = (total[:, HALF:] + half_r[k].astype(F32)).astype(BF16)
        send(block, full_r.at[k], out_mp, sem_fr.at[k], to_left)

    def end_x(k):
        total = both_cores(3, k)
        arrived(full_l.at[k], sem_fl.at[k])
        arrived(full_r.at[k], sem_fr.at[k])
        total = total + full_l[k].astype(F32) + full_r[k].astype(F32)
        if k == NY - 1:
            return total
        block = terms.at[x, ys[k], c]
        block[...] = total.astype(BF16)
        send(block, from_y.at[y], out_mp, sem_fy.at[y], at_mp(x, ys[k], c))
        return None

    first = div(mod(z + 8, NZ), 4)
    grad_tile(first)
    z_step(0, (True,))
    grad_tile(first + 1)
    z_step(0, (False,))
    lax.fori_loop(0, D // 256, share, 0)
    for j in range(NX):
        send(terms.at[order[j], :, other_c], from_core.at[j], out_mp, sem_core.at[j], to_sib)
    grad_tile(first + 3)
    z_step(1)
    arrived(from_core.at[0], sem_core.at[0])
    for k in range(NY):
        start_x(k)
    grad_tile(first + 2)
    own_over()
    z_step(2)
    arrived(from_core.at[1], sem_core.at[1])
    arrived(from_core.at[2], sem_core.at[2])
    relay_x(0)
    relay_x(1)
    z_step(3)
    relay_x(2)
    relay_x(3)
    z_step(4)
    arrived(from_core.at[3], sem_core.at[3])
    end_x(0)
    z_step(5)
    end_x(1)
    end_x(2)
    z_step(6)
    d_normed = end_x(3)
    z_step(7)
    for k in range(NY - 1):
        arrived(from_y.at[ys[k]], sem_fy.at[ys[k]])
        d_normed = d_normed + from_y[ys[k]].astype(F32)
    rows = in_ref[...].astype(F32)
    centered = rows - jnp.sum(rows, -1, keepdims=True) * (1.0 / D)
    inv = lax.rsqrt(jnp.sum(centered * centered, -1, keepdims=True) * (1.0 / D) + 1e-6)
    hat = centered * inv
    grown = d_normed * gain_ref[...]
    lean = jnp.sum(grown * hat, -1, keepdims=True) * (1.0 / D)
    ing_ref[...] = (inv * (grown - jnp.sum(grown, -1, keepdims=True) * (1.0 / D) - hat * lean)).astype(BF16)
    store_ing = pltpu.make_async_copy(ing_ref, ing_hbm, sem_ing)
    store_ing.start()

    total = grads[h, z].astype(F32)
    arrived(yh_in.at[0], sem_own)
    total = total + yh_in[0].astype(F32)
    for part in range(Z_PARTS):
        rows = pl.ds(part * PART, PART)
        arrived(zin_l.at[LEFT_STEPS - 1, 1, rows], sem_zl.at[LEFT_STEPS - 1, Z_PARTS + part])
        arrived(yh_in.at[2, rows], sem_yh.at[2, part])
    total = total + zin_l[LEFT_STEPS - 1, 1].astype(F32) + yh_in[2].astype(F32)
    for part in range(Z_PARTS):
        rows = pl.ds(part * PART, PART)
        arrived(zin_r.at[RIGHT_STEPS - 1, 1, rows], sem_zr.at[RIGHT_STEPS - 1, Z_PARTS + part])
        arrived(yh_in.at[1, rows], sem_yh.at[1, part])
    total = total + zin_r[RIGHT_STEPS - 1, 1].astype(F32) + yh_in[1].astype(F32)
    wg_ref[...] = total.reshape(OWN, 1, QKV)
    store_wg = pltpu.make_async_copy(wg_ref, wg_hbm, sem_wg)
    store_wg.start()

    for sem in (out_ag, out_mp):
        arrived(normed.at[pl.ds(0, 3)], sem)
        arrived(normed.at[3, pl.ds(0, 3)], sem)
        arrived(normed.at[3, 3, 0], sem)
    arrived(grads.at[0], out_z)
    arrived(grads.at[1, pl.ds(0, 15)], out_z)
    store_att.wait()
    store_ing.wait()
    store_wg.wait()


def local(inputs, gain, qkv_weight, d_attended):
    anywhere = pl.BlockSpec(memory_space=pl.ANY)
    dma = pltpu.SemaphoreType.DMA
    blocks = (NX, NY, NC, ROWS, D)
    attended, input_grad, weight_grad = pl.pallas_call(
        kernel,
        out_shape=(
            jax.ShapeDtypeStruct((2, IMAGE, HD), BF16),
            jax.ShapeDtypeStruct((ROWS, D), BF16),
            jax.ShapeDtypeStruct((OWN, 1, QKV), F32),
        ),
        in_specs=[anywhere] * 4,
        out_specs=(anywhere,) * 3,
        scratch_shapes=[
            pltpu.VMEM((2, IMAGE, HD), BF16),
            pltpu.VMEM((ROWS, D), BF16),
            pltpu.VMEM((OWN, 1, QKV), F32),
            pltpu.VMEM((ROWS, D), BF16),
            pltpu.VMEM((1, D), F32),
            pltpu.VMEM((D, QKV), BF16),
            pltpu.VMEM((2, IMAGE, HD), BF16),
            pltpu.VMEM(blocks, BF16),
            pltpu.VMEM((NX, IMAGE // 2, QKV), BF16),
            pltpu.VMEM((2, IMAGE, QKV), BF16),
            pltpu.VMEM((NH, NZ, OWN, QKV), BF16),
            pltpu.VMEM(blocks, BF16),
            pltpu.VMEM((NX, NY, ROWS, D), BF16),
            pltpu.VMEM((NY, ROWS, HALF), BF16),
            pltpu.VMEM((NY, ROWS, HALF), BF16),
            pltpu.VMEM((NY, ROWS, D), BF16),
            pltpu.VMEM((NY, ROWS, D), BF16),
            pltpu.VMEM((NY, ROWS, D), BF16),
            pltpu.VMEM((RIGHT_STEPS, 2, OWN, QKV), BF16),
            pltpu.VMEM((LEFT_STEPS, 2, OWN, QKV), BF16),
            pltpu.VMEM((3, OWN, QKV), BF16),
            dma, dma, dma, dma,
            dma((NY,)), dma((NY, 2)), dma((NY, 2)), dma((NY,)), dma((NY,)), dma((NY,)), dma((4,)),
            dma((RIGHT_STEPS, 2 * Z_PARTS)), dma((LEFT_STEPS, 2 * Z_PARTS)),
            dma((NX,)), dma((NY,)), dma((NY,)), dma((NY,)), dma((NY,)), dma((NY,)), dma((3, Z_PARTS)), dma, dma, dma, dma,
            dma, dma, dma,
        ],
        compiler_params=pltpu.CompilerParams(
            collective_id=0, has_side_effects=True, vmem_limit_bytes=60 * 1024 * 1024
        ),
    )(inputs, gain.reshape(1, D), qkv_weight.reshape(D, QKV), d_attended.reshape(2, IMAGE, HD))
    return (attended.reshape(GROUP, 1, HD), input_grad, weight_grad)


def solution(mesh):
    return jax.shard_map(
        local,
        mesh=mesh,
        in_specs=(P(("dp", "mp"), None), P(), P(None, "mp", None), P("dp", "mp", None)),
        out_specs=(P("dp", "mp", None), P(("dp", "mp"), None), P("dp", "mp", None)),
        check_vma=False,
    )
```

```python
import jax
import jax.numpy as jnp
from jax import lax
from jax.experimental import pallas as pl
from jax.experimental.pallas import tpu as pltpu
from jax.sharding import PartitionSpec as P

MESH = pl.DeviceIdType.MESH
STRAIGHT = (True, False, False, True)
FAR_AT = 1
Z_PARTS = 2
BF16, F32 = jnp.bfloat16, jnp.float32

NX, NY, NC, NZ, NH = 4, 4, 2, 16, 2
ROWS, D, HD = 16, 3072, 128
QKV = 3 * HD
GROUP = NX * NY * NC * ROWS
IMAGE = GROUP // 2
HALF = D // 2
OWN = D // (NZ * NH)
RIGHT_STEPS, LEFT_STEPS = NZ // 2, NZ // 2 - 1
PART = OWN // Z_PARTS
TILE = 4 * OWN


def mod(a, n):
    return lax.rem(a, jnp.int32(n))


def div(a, n):
    return lax.div(a, jnp.int32(n))


def dot(a, b, ca, cb):
    return lax.dot_general(a, b, (((ca,), (cb,)), ((), ())), preferred_element_type=F32)


def arrived(ref, sem):
    pltpu.make_async_copy(ref, ref, sem).wait()


def kernel(
    in_hbm, gain_hbm, w_hbm, do_hbm,
    att_ref, ing_ref, wg_ref,
    in_ref, gain_ref, w, do, normed, qkv, dqkv, grads, terms, from_core, half_l, half_r, full_l, full_r, from_y,
    zin_r, zin_l, yh_in,
    sem_in, sem_gain, sem_w, sem_do, sem_y, sem_xl, sem_xr, sem_xo, sem_x2l, sem_x2r, sem_sib,
    sem_zr, sem_zl, sem_core, sem_hl, sem_hr, sem_fl, sem_fr, sem_fy, sem_yh, sem_own,
    out_ag, out_z, out_mp,
):
    dp, mp = lax.axis_index("dp"), lax.axis_index("mp")
    x, y, c = div(mp, 8), mod(div(mp, 2), 4), mod(mp, 2)
    h, z = div(dp, NZ), mod(dp, NZ)
    xr, xl, xo = mod(x + 1, NX), mod(x + 3, NX), mod(x + 2, NX)
    other_c, other_h = 1 - c, 1 - h
    near = [y, y + 1 - 2 * mod(y, 2), mod(y + 2, NY), NY - 1 - y]
    middle = div(mod(y + 1, NY), 2)
    swap = middle * (near[3] - near[2])
    near[2], near[3] = near[2] + swap, near[3] - swap

    def at_mp(xx, yy, cc):
        return (dp, xx * 8 + yy * 2 + cc)

    to_right, to_left = at_mp(xr, y, c), at_mp(xl, y, c)
    to_sib, to_across = at_mp(x, y, other_c), at_mp(xo, y, c)
    to_zr, to_zl = (h * NZ + mod(z + 1, NZ), mp), (h * NZ + mod(z + NZ - 1, NZ), mp)
    over, over_zr, over_zl = ((other_h * NZ + mod(z + step, NZ), mp) for step in (0, 1, NZ - 1))

    def send(src, dst, out_sem, in_sem, device):
        pltpu.make_async_remote_copy(
            src_ref=src, dst_ref=dst, send_sem=out_sem, recv_sem=in_sem, device_id=device, device_id_type=MESH
        ).start()

    barrier = pltpu.get_barrier_semaphore()
    partners = [to_right, to_left, to_across, to_sib, to_zr, to_zl, over, over_zr, over_zl] + [at_mp(x, near[k], c) for k in (1, 2, 3)]
    for device in partners:
        pl.semaphore_signal(barrier, inc=1, device_id=device, device_id_type=MESH)
    load_in = pltpu.make_async_copy(in_hbm, in_ref, sem_in)
    load_in.start()
    load_gain = pltpu.make_async_copy(gain_hbm, gain_ref, sem_gain)
    load_gain.start()
    load_w = pltpu.make_async_copy(w_hbm, w, sem_w)
    load_w.start()
    load_do = pltpu.make_async_copy(do_hbm, do, sem_do)
    load_do.start()

    load_in.wait()
    load_gain.wait()
    rows = in_ref[...].astype(F32)
    gain = gain_ref[...]
    mean = jnp.sum(rows, -1, keepdims=True) * (1.0 / D)
    centered = rows - mean
    inv = lax.rsqrt(jnp.sum(centered * centered, -1, keepdims=True) * (1.0 / D) + 1e-6)
    normed[x, y, c] = (centered * inv * gain).astype(BF16)

    pl.semaphore_wait(barrier, len(partners))

    def to_sibling(ref, slot):
        send(ref, ref, out_ag, sem_sib.at[slot], to_sib)

    pieces = (pl.ds(0, HALF), pl.ds(HALF, HALF))

    def along_x(k):
        yy = near[k]
        block = normed.at[x, yy, c]
        for right, p in ((True, 0), (False, 1), (True, 1), (False, 0)):
            part = block.at[:, pieces[p]]
            sem, device = (sem_xl, to_right) if right else (sem_xr, to_left)
            send(part, part, out_ag, sem.at[yy, p], device)
        if k == 0:
            send(block, block, out_ag, sem_xo.at[yy], to_across)

    def along_y(k):
        send(own, own, out_ag, sem_y.at[y], at_mp(x, near[k], c))

    def past_middle():
        block = normed.at[x, near[2], c]
        send(block, block, out_ag, sem_y.at[near[2]], at_mp(x, near[1], c))

    def far_across():
        block = normed.at[xo, y, c]
        send(block, block, out_ag, sem_xo.at[y], at_mp(x, NY - 1 - y, c))
        send(block, block, out_ag, sem_xo.at[y], at_mp(x, mod(y + 2, NY), c))

    def pass_on(k):
        yy = near[k]
        if not STRAIGHT[k]:
            part = normed.at[xl, yy, c, :, pieces[0]]
            arrived(part, sem_xl.at[yy, 0])
            send(part, part, out_ag, sem_x2l.at[yy], to_right)
            part = normed.at[xr, yy, c, :, pieces[1]]
            arrived(part, sem_xr.at[yy, 1])
            send(part, part, out_ag, sem_x2r.at[yy], to_left)

    def finish_x(k):
        yy = near[k]
        if STRAIGHT[k]:
            arrived(normed.at[xl, yy, c, :, pieces[0]], sem_xl.at[yy, 0])
            arrived(normed.at[xr, yy, c, :, pieces[1]], sem_xr.at[yy, 1])
        arrived(normed.at[xl, yy, c, :, pieces[1]], sem_xl.at[yy, 1])
        to_sibling(normed.at[xl, yy, c], 1)
        arrived(normed.at[xr, yy, c, :, pieces[0]], sem_xr.at[yy, 0])
        to_sibling(normed.at[xr, yy, c], 2)

    def second(k):
        yy = near[k]
        if STRAIGHT[k]:
            block = normed.at[xo, yy, c]
            arrived(block, sem_xo.at[yy])
            to_sibling(block, 3)
            return
        for p, sem in ((0, sem_x2l), (1, sem_x2r)):
            part = normed.at[xo, yy, c, :, pieces[p]]
            arrived(part, sem.at[yy])
            to_sibling(part, 3)

    own = normed.at[x, y, c]
    along_y(1)
    along_y(2)
    along_x(0)
    pl.when(middle == 0)(lambda: along_y(3))
    to_sibling(own, 0)
    for k in range(NY):
        if k + 1 < NY:
            yy = near[k + 1]
            arrived(normed.at[x, yy, c], sem_y.at[yy])
            if k + 1 == 2:
                pl.when(middle == 1)(past_middle)
            along_x(k + 1)
            to_sibling(normed.at[x, yy, c], 0)
        pass_on(k)
        if k > 0:
            finish_x(k - 1)
        if k == FAR_AT:
            second(0)
            pl.when(middle == 0)(far_across)

    def bundle(xx, slot):
        arrived(normed.at[xx, :, other_c], sem_sib.at[slot])

    def project(xx):
        qkv[xx] = dot(normed[xx].reshape(IMAGE // 2, D), w[...], 1, 0).astype(BF16)

    def attend(a):
        block = qkv[pl.ds(2 * a, 2)].reshape(IMAGE, QKV)
        q, k, v = block[:, :HD], block[:, HD : 2 * HD], block[:, 2 * HD :]
        d_out = do[a]
        scale = HD ** (-0.5)
        scores = dot(q, k, 1, 1) * scale
        expo = jnp.exp(scores - jnp.max(scores, -1, keepdims=True))
        probs = expo / jnp.sum(expo, -1, keepdims=True)
        low = probs.astype(BF16)
        att_ref[a] = dot(low, v, 1, 0).astype(BF16)
        d_probs = dot(d_out, v, 1, 1)
        dqkv[a, :, 2 * HD :] = dot(low, d_out, 0, 0).astype(BF16)
        d_scores = (probs * (d_probs - jnp.sum(d_probs * probs, -1, keepdims=True)) * scale).astype(BF16)
        dqkv[a, :, :HD] = dot(d_scores, k, 1, 0).astype(BF16)
        dqkv[a, :, HD : 2 * HD] = dot(d_scores, q, 0, 0).astype(BF16)

    image = div(x, 2)
    mate = x + 1 - 2 * mod(x, 2)
    load_w.wait()
    load_do.wait()
    bundle(x, 0)
    project(x)
    finish_x(NY - 1)
    second(1)
    second(2)
    bundle(xl, 1)
    bundle(xr, 2)
    project(mate)
    project(mod(mate + 2, NX))
    second(3)
    attend(image)
    bundle(xo, 3)
    project(xo)
    attend(1 - image)

    def grad_tile(t):
        u = mod(t, 4)
        d_all = dqkv[...].reshape(GROUP, QKV)
        for hh in range(NH):
            cols = pl.ds(pl.multiple_of((u + 4 * hh) * TILE, 128), TILE)
            tile = normed[:, :, :, :, cols].reshape(GROUP, TILE)
            grads[hh, pl.ds(4 * u, 4)] = dot(tile, d_all, 0, 0).astype(BF16).reshape(4, OWN, QKV)

    def z_part(s, sub, part, right):
        zz = mod(z + 8 - s + NZ, NZ) if right else mod(z + 9 + s, NZ)
        came, sem, device = (zin_r, sem_zr, to_zr) if right else (zin_l, sem_zl, to_zl)
        rows = pl.ds(part * PART, PART)
        block = grads.at[(other_h, h)[sub], zz, rows]
        if s > 0:
            arrived(came.at[s - 1, sub, rows], sem.at[s - 1, sub * Z_PARTS + part])
            block[...] = (block[...].astype(F32) + came[s - 1, sub, rows].astype(F32)).astype(BF16)
        last = s == (RIGHT_STEPS if right else LEFT_STEPS) - 1
        if last and sub == 0:
            slot = 1 if right else 2
            send(block, yh_in.at[slot, rows], out_z, sem_yh.at[slot, part], over_zr if right else over_zl)
        else:
            send(block, came.at[s, sub, rows], out_z, sem.at[s, sub * Z_PARTS + part], device)

    def z_step(s, ways=(True, False)):
        for sub in range(2):
            for part in range(Z_PARTS):
                for right in ways:
                    if right or s < LEFT_STEPS:
                        z_part(s, sub, part, right)

    def own_over():
        block = grads.at[other_h, z]
        send(block, yh_in.at[0], out_z, sem_own, over)

    def share(j, carry):
        cols = pl.ds(pl.multiple_of(j * 256, 256), 256)
        out = dot(dqkv[...].reshape(GROUP, QKV), w[cols, :], 1, 1).astype(BF16)
        terms[:, :, :, :, cols] = out.reshape(NX, NY, NC, ROWS, 256)
        return carry

    order = (xo, xr, xl, x)
    ys = [mod(y + 1, NY), mod(y + 2, NY), mod(y + 3, NY), y]

    def both_cores(j, k):
        return terms[order[j], ys[k], c].astype(F32) + from_core[j, ys[k]].astype(F32)

    def start_x(k):
        block = terms.at[xo, ys[k], c]
        block[...] = both_cores(0, k).astype(BF16)
        send(block.at[:, pl.ds(0, HALF)], half_l.at[k], out_mp, sem_hl.at[k], to_right)
        send(block.at[:, pl.ds(HALF, HALF)], half_r.at[k], out_mp, sem_hr.at[k], to_left)

    def relay_x(k):
        total = both_cores(1, k)
        block = terms.at[xr, ys[k], c]
        arrived(half_l.at[k], sem_hl.at[k])
        block[:, :HALF] = (total[:, :HALF] + half_l[k].astype(F32)).astype(BF16)
        block[:, HALF:] = total[:, HALF:].astype(BF16)
        send(block, full_l.at[k], out_mp, sem_fl.at[k], to_right)
        total = both_cores(2, k)
        block = terms.at[xl, ys[k], c]
        arrived(half_r.at[k], sem_hr.at[k])
        block[:, :HALF] = total[:, :HALF].astype(BF16)
        block[:, HALF:] = (total[:, HALF:] + half_r[k].astype(F32)).astype(BF16)
        send(block, full_r.at[k], out_mp, sem_fr.at[k], to_left)

    def end_x(k):
        total = both_cores(3, k)
        arrived(full_l.at[k], sem_fl.at[k])
        arrived(full_r.at[k], sem_fr.at[k])
        total = total + full_l[k].astype(F32) + full_r[k].astype(F32)
        if k == NY - 1:
            return total
        block = terms.at[x, ys[k], c]
        block[...] = total.astype(BF16)
        send(block, from_y.at[y], out_mp, sem_fy.at[y], at_mp(x, ys[k], c))
        return None

    first = div(mod(z + 8, NZ), 4)
    grad_tile(first)
    z_step(0, (True,))
    grad_tile(first + 1)
    z_step(0, (False,))
    lax.fori_loop(0, D // 256, share, 0)
    for j in range(NX):
        send(terms.at[order[j], :, other_c], from_core.at[j], out_mp, sem_core.at[j], to_sib)
    grad_tile(first + 3)
    z_step(1)
    arrived(from_core.at[0], sem_core.at[0])
    for k in range(NY):
        start_x(k)
    grad_tile(first + 2)
    own_over()
    z_step(2)
    arrived(from_core.at[1], sem_core.at[1])
    arrived(from_core.at[2], sem_core.at[2])
    relay_x(0)
    relay_x(1)
    z_step(3)
    relay_x(2)
    relay_x(3)
    z_step(4)
    arrived(from_core.at[3], sem_core.at[3])
    end_x(0)
    z_step(5)
    end_x(1)
    end_x(2)
    z_step(6)
    d_normed = end_x(3)
    z_step(7)
    for k in range(NY - 1):
        arrived(from_y.at[ys[k]], sem_fy.at[ys[k]])
        d_normed = d_normed + from_y[ys[k]].astype(F32)
    rows = in_ref[...].astype(F32)
    centered = rows - jnp.sum(rows, -1, keepdims=True) * (1.0 / D)
    inv = lax.rsqrt(jnp.sum(centered * centered, -1, keepdims=True) * (1.0 / D) + 1e-6)
    hat = centered * inv
    grown = d_normed * gain_ref[...]
    lean = jnp.sum(grown * hat, -1, keepdims=True) * (1.0 / D)
    ing_ref[...] = (inv * (grown - jnp.sum(grown, -1, keepdims=True) * (1.0 / D) - hat * lean)).astype(BF16)

    total = grads[h, z].astype(F32)
    arrived(yh_in.at[0], sem_own)
    total = total + yh_in[0].astype(F32)
    for part in range(Z_PARTS):
        rows = pl.ds(part * PART, PART)
        arrived(zin_l.at[LEFT_STEPS - 1, 1, rows], sem_zl.at[LEFT_STEPS - 1, Z_PARTS + part])
        arrived(yh_in.at[2, rows], sem_yh.at[2, part])
    total = total + zin_l[LEFT_STEPS - 1, 1].astype(F32) + yh_in[2].astype(F32)
    for part in range(Z_PARTS):
        rows = pl.ds(part * PART, PART)
        arrived(zin_r.at[RIGHT_STEPS - 1, 1, rows], sem_zr.at[RIGHT_STEPS - 1, Z_PARTS + part])
        arrived(yh_in.at[1, rows], sem_yh.at[1, part])
    total = total + zin_r[RIGHT_STEPS - 1, 1].astype(F32) + yh_in[1].astype(F32)
    wg_ref[...] = total.reshape(OWN, 1, QKV)

    arrived(normed.at[pl.ds(0, 3)], out_mp)
    arrived(normed.at[3, pl.ds(0, 3)], out_mp)
    arrived(normed.at[3, 3, 0], out_mp)
    arrived(normed.at[pl.ds(0, 3)], out_ag)
    arrived(normed.at[3, pl.ds(0, 3)], out_ag)
    pl.when(middle == 0)(lambda: arrived(normed.at[3, 3], out_ag))
    arrived(grads.at[0], out_z)
    arrived(grads.at[1, pl.ds(0, 15)], out_z)


def local(inputs, gain, qkv_weight, d_attended):
    anywhere = pl.BlockSpec(memory_space=pl.ANY)
    dma = pltpu.SemaphoreType.DMA
    blocks = (NX, NY, NC, ROWS, D)
    attended, input_grad, weight_grad = pl.pallas_call(
        kernel,
        out_shape=(
            pltpu.VMEM((2, IMAGE, HD), BF16),
            pltpu.VMEM((ROWS, D), BF16),
            pltpu.VMEM((OWN, 1, QKV), F32),
        ),
        in_specs=[pl.BlockSpec(memory_space=pltpu.HBM)] * 4,
        out_specs=(pl.BlockSpec(memory_space=pltpu.VMEM),) * 3,
        scratch_shapes=[
            pltpu.VMEM((ROWS, D), BF16),
            pltpu.VMEM((1, D), F32),
            pltpu.VMEM((D, QKV), BF16),
            pltpu.VMEM((2, IMAGE, HD), BF16),
            pltpu.VMEM(blocks, BF16),
            pltpu.VMEM((NX, IMAGE // 2, QKV), BF16),
            pltpu.VMEM((2, IMAGE, QKV), BF16),
            pltpu.VMEM((NH, NZ, OWN, QKV), BF16),
            pltpu.VMEM(blocks, BF16),
            pltpu.VMEM((NX, NY, ROWS, D), BF16),
            pltpu.VMEM((NY, ROWS, HALF), BF16),
            pltpu.VMEM((NY, ROWS, HALF), BF16),
            pltpu.VMEM((NY, ROWS, D), BF16),
            pltpu.VMEM((NY, ROWS, D), BF16),
            pltpu.VMEM((NY, ROWS, D), BF16),
            pltpu.VMEM((RIGHT_STEPS, 2, OWN, QKV), BF16),
            pltpu.VMEM((LEFT_STEPS, 2, OWN, QKV), BF16),
            pltpu.VMEM((3, OWN, QKV), BF16),
            dma, dma, dma, dma,
            dma((NY,)), dma((NY, 2)), dma((NY, 2)), dma((NY,)), dma((NY,)), dma((NY,)), dma((4,)),
            dma((RIGHT_STEPS, 2 * Z_PARTS)), dma((LEFT_STEPS, 2 * Z_PARTS)),
            dma((NX,)), dma((NY,)), dma((NY,)), dma((NY,)), dma((NY,)), dma((NY,)), dma((3, Z_PARTS)), dma,
            dma, dma, dma,
        ],
        compiler_params=pltpu.CompilerParams(
            collective_id=0, has_side_effects=True, vmem_limit_bytes=60 * 1024 * 1024
        ),
    )(inputs, gain.reshape(1, D), qkv_weight.reshape(D, QKV), d_attended.reshape(2, IMAGE, HD))
    return (attended.reshape(GROUP, 1, HD), input_grad, weight_grad)


def solution(mesh):
    return jax.shard_map(
        local,
        mesh=mesh,
        in_specs=(P(("dp", "mp"), None), P(), P(None, "mp", None), P("dp", "mp", None)),
        out_specs=(P("dp", "mp", None), P(("dp", "mp"), None), P("dp", "mp", None)),
        check_vma=False,
    )
```

```python
import jax
import jax.numpy as jnp
from jax import lax
from jax.experimental import pallas as pl
from jax.experimental.pallas import tpu as pltpu
from jax.sharding import PartitionSpec as P

MESH = pl.DeviceIdType.MESH
STRAIGHT = (True, False, False, True)
FAR_AT = 1
Z_PARTS = 2
BF16, F32 = jnp.bfloat16, jnp.float32

NX, NY, NC, NZ, NH = 4, 4, 2, 16, 2
ROWS, D, HD = 16, 3072, 128
QKV = 3 * HD
GROUP = NX * NY * NC * ROWS
IMAGE = GROUP // 2
HALF = D // 2
OWN = D // (NZ * NH)
RIGHT_STEPS, LEFT_STEPS = NZ // 2, NZ // 2 - 1
PART = OWN // Z_PARTS
TILE = 4 * OWN


def mod(a, n):
    return lax.rem(a, jnp.int32(n))


def div(a, n):
    return lax.div(a, jnp.int32(n))


def dot(a, b, ca, cb):
    return lax.dot_general(a, b, (((ca,), (cb,)), ((), ())), preferred_element_type=F32)


def arrived(ref, sem):
    pltpu.make_async_copy(ref, ref, sem).wait()


def kernel(
    in_hbm, gain_hbm, w_hbm, do_hbm,
    att_ref, ing_ref, wg_ref,
    in_ref, gain_ref, w, do, normed, qkv, dqkv, grads, terms, from_core, half_l, half_r, full_l, full_r, from_y,
    zin_r, zin_l, yh_in,
    sem_in, sem_gain, sem_w, sem_do, sem_y, sem_xl, sem_xr, sem_xo, sem_x2l, sem_x2r, sem_sib,
    sem_zr, sem_zl, sem_core, sem_hl, sem_hr, sem_fl, sem_fr, sem_fy, sem_yh, sem_own,
    out_ag, out_z, out_mp,
):
    dp, mp = lax.axis_index("dp"), lax.axis_index("mp")
    x, y, c = div(mp, 8), mod(div(mp, 2), 4), mod(mp, 2)
    h, z = div(dp, NZ), mod(dp, NZ)
    xr, xl, xo = mod(x + 1, NX), mod(x + 3, NX), mod(x + 2, NX)
    other_c, other_h = 1 - c, 1 - h
    near = [y, y + 1 - 2 * mod(y, 2), mod(y + 2, NY), NY - 1 - y]
    middle = div(mod(y + 1, NY), 2)
    swap = middle * (near[3] - near[2])
    near[2], near[3] = near[2] + swap, near[3] - swap

    def at_mp(xx, yy, cc):
        return (dp, xx * 8 + yy * 2 + cc)

    to_right, to_left = at_mp(xr, y, c), at_mp(xl, y, c)
    to_sib, to_across = at_mp(x, y, other_c), at_mp(xo, y, c)
    to_zr, to_zl = (h * NZ + mod(z + 1, NZ), mp), (h * NZ + mod(z + NZ - 1, NZ), mp)
    over, over_zr, over_zl = ((other_h * NZ + mod(z + step, NZ), mp) for step in (0, 1, NZ - 1))

    def send(src, dst, out_sem, in_sem, device):
        pltpu.make_async_remote_copy(
            src_ref=src, dst_ref=dst, send_sem=out_sem, recv_sem=in_sem, device_id=device, device_id_type=MESH
        ).start()

    barrier = pltpu.get_barrier_semaphore()
    partners = [to_right, to_left, to_across, to_sib, to_zr, to_zl, over, over_zr, over_zl] + [at_mp(x, near[k], c) for k in (1, 2, 3)]
    for device in partners:
        pl.semaphore_signal(barrier, inc=1, device_id=device, device_id_type=MESH)
    load_in = pltpu.make_async_copy(in_hbm, in_ref, sem_in)
    load_in.start()
    load_gain = pltpu.make_async_copy(gain_hbm, gain_ref, sem_gain)
    load_gain.start()
    load_w = pltpu.make_async_copy(w_hbm, w, sem_w)
    load_w.start()
    load_do = pltpu.make_async_copy(do_hbm, do, sem_do)
    load_do.start()

    load_in.wait()
    load_gain.wait()
    rows = in_ref[...].astype(F32)
    gain = gain_ref[...]
    mean = jnp.sum(rows, -1, keepdims=True) * (1.0 / D)
    centered = rows - mean
    inv = lax.rsqrt(jnp.sum(centered * centered, -1, keepdims=True) * (1.0 / D) + 1e-6)
    normed[x, y, c] = (centered * inv * gain).astype(BF16)

    pl.semaphore_wait(barrier, len(partners))

    def to_sibling(ref, slot):
        send(ref, ref, out_ag, sem_sib.at[slot], to_sib)

    pieces = (pl.ds(0, HALF), pl.ds(HALF, HALF))

    def along_x(k):
        yy = near[k]
        block = normed.at[x, yy, c]
        for right, p in ((True, 0), (False, 1), (True, 1), (False, 0)):
            part = block.at[:, pieces[p]]
            sem, device = (sem_xl, to_right) if right else (sem_xr, to_left)
            send(part, part, out_ag, sem.at[yy, p], device)
        if k == 0:
            send(block, block, out_ag, sem_xo.at[yy], to_across)

    def along_y(k):
        send(own, own, out_ag, sem_y.at[y], at_mp(x, near[k], c))

    def past_middle():
        block = normed.at[x, near[2], c]
        send(block, block, out_ag, sem_y.at[near[2]], at_mp(x, near[1], c))

    def far_across():
        block = normed.at[xo, y, c]
        send(block, block, out_ag, sem_xo.at[y], at_mp(x, NY - 1 - y, c))
        send(block, block, out_ag, sem_xo.at[y], at_mp(x, mod(y + 2, NY), c))

    def pass_on(k):
        yy = near[k]
        if not STRAIGHT[k]:
            part = normed.at[xl, yy, c, :, pieces[0]]
            arrived(part, sem_xl.at[yy, 0])
            send(part, part, out_ag, sem_x2l.at[yy], to_right)
            part = normed.at[xr, yy, c, :, pieces[1]]
            arrived(part, sem_xr.at[yy, 1])
            send(part, part, out_ag, sem_x2r.at[yy], to_left)

    def finish_x(k):
        yy = near[k]
        if STRAIGHT[k]:
            arrived(normed.at[xl, yy, c, :, pieces[0]], sem_xl.at[yy, 0])
            arrived(normed.at[xr, yy, c, :, pieces[1]], sem_xr.at[yy, 1])
        arrived(normed.at[xl, yy, c, :, pieces[1]], sem_xl.at[yy, 1])
        to_sibling(normed.at[xl, yy, c], 1)
        arrived(normed.at[xr, yy, c, :, pieces[0]], sem_xr.at[yy, 0])
        to_sibling(normed.at[xr, yy, c], 2)

    def second(k):
        yy = near[k]
        if STRAIGHT[k]:
            block = normed.at[xo, yy, c]
            arrived(block, sem_xo.at[yy])
            to_sibling(block, 3)
            return
        for p, sem in ((0, sem_x2l), (1, sem_x2r)):
            part = normed.at[xo, yy, c, :, pieces[p]]
            arrived(part, sem.at[yy])
            to_sibling(part, 3)

    own = normed.at[x, y, c]
    along_y(1)
    along_y(2)
    along_x(0)
    pl.when(middle == 0)(lambda: along_y(3))
    to_sibling(own, 0)
    for k in range(NY):
        if k + 1 < NY:
            yy = near[k + 1]
            arrived(normed.at[x, yy, c], sem_y.at[yy])
            if k + 1 == 2:
                pl.when(middle == 1)(past_middle)
            along_x(k + 1)
            to_sibling(normed.at[x, yy, c], 0)
        pass_on(k)
        if k > 0:
            finish_x(k - 1)
        if k == FAR_AT:
            second(0)
            pl.when(middle == 0)(far_across)

    def bundle(xx, slot):
        arrived(normed.at[xx, :, other_c], sem_sib.at[slot])

    def project(xx):
        qkv[xx] = dot(normed[xx].reshape(IMAGE // 2, D), w[...], 1, 0).astype(BF16)

    def attend(a):
        block = qkv[pl.ds(2 * a, 2)].reshape(IMAGE, QKV)
        q, k, v = block[:, :HD], block[:, HD : 2 * HD], block[:, 2 * HD :]
        d_out = do[a]
        scale = HD ** (-0.5)
        scores = dot(q, k, 1, 1) * scale
        expo = jnp.exp(scores - jnp.max(scores, -1, keepdims=True))
        probs = expo / jnp.sum(expo, -1, keepdims=True)
        low = probs.astype(BF16)
        att_ref[a] = dot(low, v, 1, 0).astype(BF16)
        d_probs = dot(d_out, v, 1, 1)
        dqkv[a, :, 2 * HD :] = dot(low, d_out, 0, 0).astype(BF16)
        d_scores = (probs * (d_probs - jnp.sum(d_probs * probs, -1, keepdims=True)) * scale).astype(BF16)
        dqkv[a, :, :HD] = dot(d_scores, k, 1, 0).astype(BF16)
        dqkv[a, :, HD : 2 * HD] = dot(d_scores, q, 0, 0).astype(BF16)

    image = div(x, 2)
    mate = x + 1 - 2 * mod(x, 2)
    load_w.wait()
    load_do.wait()
    bundle(x, 0)
    project(x)
    finish_x(NY - 1)
    second(1)
    second(2)
    bundle(xl, 1)
    bundle(xr, 2)
    project(mate)
    project(mod(mate + 2, NX))
    second(3)
    attend(image)
    bundle(xo, 3)
    project(xo)
    attend(1 - image)

    def grad_tile(t):
        u = mod(t, 4)
        d_all = dqkv[...].reshape(GROUP, QKV)
        for hh in range(NH):
            cols = pl.ds(pl.multiple_of((u + 4 * hh) * TILE, 128), TILE)
            tile = normed[:, :, :, :, cols].reshape(GROUP, TILE)
            grads[hh, pl.ds(4 * u, 4)] = dot(tile, d_all, 0, 0).astype(BF16).reshape(4, OWN, QKV)

    def z_part(s, sub, part, right):
        zz = mod(z + 8 - s + NZ, NZ) if right else mod(z + 9 + s, NZ)
        came, sem, device = (zin_r, sem_zr, to_zr) if right else (zin_l, sem_zl, to_zl)
        rows = pl.ds(part * PART, PART)
        block = grads.at[(other_h, h)[sub], zz, rows]
        if s > 0:
            arrived(came.at[s - 1, sub, rows], sem.at[s - 1, sub * Z_PARTS + part])
            block[...] = (block[...].astype(F32) + came[s - 1, sub, rows].astype(F32)).astype(BF16)
        last = s == (RIGHT_STEPS if right else LEFT_STEPS) - 1
        if last and sub == 0:
            slot = 1 if right else 2
            send(block, yh_in.at[slot, rows], out_z, sem_yh.at[slot, part], over_zr if right else over_zl)
        else:
            send(block, came.at[s, sub, rows], out_z, sem.at[s, sub * Z_PARTS + part], device)

    def z_step(s, ways):
        for sub in range(2):
            z_half(s, sub, ways)

    def z_half(s, sub, ways=(True, False)):
        for part in range(Z_PARTS):
            for right in ways:
                if right or s < LEFT_STEPS:
                    z_part(s, sub, part, right)

    def own_over():
        block = grads.at[other_h, z]
        send(block, yh_in.at[0], out_z, sem_own, over)

    def share(j, carry):
        cols = pl.ds(j * 512, 512)
        out = dot(dqkv[...].reshape(GROUP, QKV), w[cols, :], 1, 1).astype(BF16)
        terms[:, :, :, :, cols] = out.reshape(NX, NY, NC, ROWS, 512)
        return carry

    order = (xo, xr, xl, x)
    ys = [mod(y + 1, NY), mod(y + 2, NY), mod(y + 3, NY), y]

    def both_cores(j, k):
        return terms[order[j], ys[k], c].astype(F32) + from_core[j, ys[k]].astype(F32)

    def start_x(k):
        block = terms.at[xo, ys[k], c]
        block[...] = both_cores(0, k).astype(BF16)
        send(block.at[:, pl.ds(0, HALF)], half_l.at[k], out_mp, sem_hl.at[k], to_right)
        send(block.at[:, pl.ds(HALF, HALF)], half_r.at[k], out_mp, sem_hr.at[k], to_left)

    def relay_x(k):
        total = both_cores(1, k)
        block = terms.at[xr, ys[k], c]
        arrived(half_l.at[k], sem_hl.at[k])
        block[:, :HALF] = (total[:, :HALF] + half_l[k].astype(F32)).astype(BF16)
        block[:, HALF:] = total[:, HALF:].astype(BF16)
        send(block, full_l.at[k], out_mp, sem_fl.at[k], to_right)
        total = both_cores(2, k)
        block = terms.at[xl, ys[k], c]
        arrived(half_r.at[k], sem_hr.at[k])
        block[:, :HALF] = total[:, :HALF].astype(BF16)
        block[:, HALF:] = (total[:, HALF:] + half_r[k].astype(F32)).astype(BF16)
        send(block, full_r.at[k], out_mp, sem_fr.at[k], to_left)

    def end_x(k):
        total = both_cores(3, k)
        arrived(full_l.at[k], sem_fl.at[k])
        arrived(full_r.at[k], sem_fr.at[k])
        total = total + full_l[k].astype(F32) + full_r[k].astype(F32)
        if k == NY - 1:
            return total
        block = terms.at[x, ys[k], c]
        block[...] = total.astype(BF16)
        send(block, from_y.at[y], out_mp, sem_fy.at[y], at_mp(x, ys[k], c))
        return None

    first = div(mod(z + 8, NZ), 4)
    grad_tile(first)
    z_step(0, (True,))
    grad_tile(first + 1)
    z_step(0, (False,))
    for j in range(D // 512):
        share(j, 0)
    for j in range(NX):
        send(terms.at[order[j], :, other_c], from_core.at[j], out_mp, sem_core.at[j], to_sib)
    grad_tile(first + 3)
    z_half(1, 0)
    arrived(from_core.at[0], sem_core.at[0])
    start_x(0)
    start_x(1)
    z_half(1, 1)
    start_x(2)
    start_x(3)
    z_half(2, 0)
    grad_tile(first + 2)
    own_over()
    z_half(2, 1)
    arrived(from_core.at[1], sem_core.at[1])
    arrived(from_core.at[2], sem_core.at[2])
    relay_x(0)
    relay_x(1)
    z_half(3, 0)
    relay_x(2)
    z_half(3, 1)
    relay_x(3)
    arrived(from_core.at[3], sem_core.at[3])
    z_half(4, 0)
    z_half(4, 1)
    end_x(0)
    z_half(5, 0)
    end_x(1)
    z_half(5, 1)
    end_x(2)
    z_half(6, 0)
    z_half(6, 1)
    d_normed = end_x(3)
    z_half(7, 0)
    z_half(7, 1)
    for k in range(NY - 1):
        arrived(from_y.at[ys[k]], sem_fy.at[ys[k]])
        d_normed = d_normed + from_y[ys[k]].astype(F32)
    rows = in_ref[...].astype(F32)
    centered = rows - jnp.sum(rows, -1, keepdims=True) * (1.0 / D)
    inv = lax.rsqrt(jnp.sum(centered * centered, -1, keepdims=True) * (1.0 / D) + 1e-6)
    hat = centered * inv
    grown = d_normed * gain_ref[...]
    lean = jnp.sum(grown * hat, -1, keepdims=True) * (1.0 / D)
    ing_ref[...] = (inv * (grown - jnp.sum(grown, -1, keepdims=True) * (1.0 / D) - hat * lean)).astype(BF16)

    total = grads[h, z].astype(F32)
    arrived(yh_in.at[0], sem_own)
    total = total + yh_in[0].astype(F32)
    for part in range(Z_PARTS):
        rows = pl.ds(part * PART, PART)
        arrived(zin_l.at[LEFT_STEPS - 1, 1, rows], sem_zl.at[LEFT_STEPS - 1, Z_PARTS + part])
        arrived(yh_in.at[2, rows], sem_yh.at[2, part])
    total = total + zin_l[LEFT_STEPS - 1, 1].astype(F32) + yh_in[2].astype(F32)
    for part in range(Z_PARTS):
        rows = pl.ds(part * PART, PART)
        arrived(zin_r.at[RIGHT_STEPS - 1, 1, rows], sem_zr.at[RIGHT_STEPS - 1, Z_PARTS + part])
        arrived(yh_in.at[1, rows], sem_yh.at[1, part])
    total = total + zin_r[RIGHT_STEPS - 1, 1].astype(F32) + yh_in[1].astype(F32)
    wg_ref[...] = total.reshape(OWN, 1, QKV)

    arrived(normed.at[pl.ds(0, 3)], out_mp)
    arrived(normed.at[3, pl.ds(0, 3)], out_mp)
    arrived(normed.at[3, 3, 0], out_mp)
    arrived(normed.at[pl.ds(0, 3)], out_ag)
    arrived(normed.at[3, pl.ds(0, 3)], out_ag)
    pl.when(middle == 0)(lambda: arrived(normed.at[3, 3], out_ag))
    arrived(grads.at[0], out_z)
    arrived(grads.at[1, pl.ds(0, 15)], out_z)


def local(inputs, gain, qkv_weight, d_attended):
    anywhere = pl.BlockSpec(memory_space=pl.ANY)
    dma = pltpu.SemaphoreType.DMA
    blocks = (NX, NY, NC, ROWS, D)
    attended, input_grad, weight_grad = pl.pallas_call(
        kernel,
        out_shape=(
            pltpu.VMEM((2, IMAGE, HD), BF16),
            pltpu.VMEM((ROWS, D), BF16),
            pltpu.VMEM((OWN, 1, QKV), F32),
        ),
        in_specs=[pl.BlockSpec(memory_space=pltpu.HBM)] * 4,
        out_specs=(pl.BlockSpec(memory_space=pltpu.VMEM),) * 3,
        scratch_shapes=[
            pltpu.VMEM((ROWS, D), BF16),
            pltpu.VMEM((1, D), F32),
            pltpu.VMEM((D, QKV), BF16),
            pltpu.VMEM((2, IMAGE, HD), BF16),
            pltpu.VMEM(blocks, BF16),
            pltpu.VMEM((NX, IMAGE // 2, QKV), BF16),
            pltpu.VMEM((2, IMAGE, QKV), BF16),
            pltpu.VMEM((NH, NZ, OWN, QKV), BF16),
            pltpu.VMEM(blocks, BF16),
            pltpu.VMEM((NX, NY, ROWS, D), BF16),
            pltpu.VMEM((NY, ROWS, HALF), BF16),
            pltpu.VMEM((NY, ROWS, HALF), BF16),
            pltpu.VMEM((NY, ROWS, D), BF16),
            pltpu.VMEM((NY, ROWS, D), BF16),
            pltpu.VMEM((NY, ROWS, D), BF16),
            pltpu.VMEM((RIGHT_STEPS, 2, OWN, QKV), BF16),
            pltpu.VMEM((LEFT_STEPS, 2, OWN, QKV), BF16),
            pltpu.VMEM((3, OWN, QKV), BF16),
            dma, dma, dma, dma,
            dma((NY,)), dma((NY, 2)), dma((NY, 2)), dma((NY,)), dma((NY,)), dma((NY,)), dma((4,)),
            dma((RIGHT_STEPS, 2 * Z_PARTS)), dma((LEFT_STEPS, 2 * Z_PARTS)),
            dma((NX,)), dma((NY,)), dma((NY,)), dma((NY,)), dma((NY,)), dma((NY,)), dma((3, Z_PARTS)), dma,
            dma, dma, dma,
        ],
        compiler_params=pltpu.CompilerParams(
            collective_id=0, has_side_effects=True, vmem_limit_bytes=60 * 1024 * 1024
        ),
    )(inputs, gain.reshape(1, D), qkv_weight.reshape(D, QKV), d_attended.reshape(2, IMAGE, HD))
    return (attended.reshape(GROUP, 1, HD), input_grad, weight_grad)


def solution(mesh):
    return jax.shard_map(
        local,
        mesh=mesh,
        in_specs=(P(("dp", "mp"), None), P(), P(None, "mp", None), P("dp", "mp", None)),
        out_specs=(P("dp", "mp", None), P(("dp", "mp"), None), P("dp", "mp", None)),
        check_vma=False,
    )
```
